256 devices in a mesh: row: 8 (over z), col: 32 (over y, x, core).
Axes of the slice: x: 4, y: 4, z: 8, core: 2. Of those that a mesh axis runs over, the one named last changes fastest.
Arguments:
- queries: bfloat16 [32, 1024, 6144], P('col', 'row'), may hold values from -6 to 6
- keys: bfloat16 [32, 1024, 6144], P('col', 'row'), may hold values from -6 to 6
- values: bfloat16 [32, 1024, 6144], P('col', 'row'), may hold values from -6 to 6
- query_gain: float32 [6144], replicated, may hold values from 1 to 2.2
- key_gain: float32 [6144], replicated, may hold values from 1 to 2.2
- cotangent: bfloat16 [32, 1024, 6144], P('col', 'row'), may hold values from -18 to 18
Outputs:
- attended: bfloat16 [32, 1024, 6144], P('col', 'row')
- query_grad: bfloat16 [32, 1024, 6144], P('col', 'row')
- key_grad: bfloat16 [32, 1024, 6144], P('col', 'row')
- value_grad: bfloat16 [32, 1024, 6144], P('col', 'row')
- query_gain_grad: float32 [6144], replicated
- key_gain_grad: float32 [6144], replicated
The draws below stay inside these ranges and needn't reach their ends.
All inputs are finite; a program needn't handle non-finite values.
Results may differ from the reference program's by a relative error of at most 0.012.
The reference program's roundings to bfloat16 on the way (of `weights_low` and `score_grad`) count: a program that leaves them out, or rounds other values in their place, can miss the bound.
Values may be sent and summed in bfloat16 or wider, within the bound.
A program may use at most 128 MiB of HBM per device.

```python
import math
import jax
import jax.numpy as jnp
from jax import lax

HEADS = 48
HD = 128
D = 6144
LENGTH = 1024
VIEWS = 32
TOKENS = 32768


def draw_cotangent(key, part):
    key = jax.random.fold_in(key, 7)
    normal_part = jnp.clip(jax.random.normal(key, (VIEWS, LENGTH, HEADS * HD), jnp.float32), -4.0, 4.0)
    position = jnp.arange(VIEWS, dtype=jnp.float32)[:, None] * LENGTH + jnp.arange(LENGTH, dtype=jnp.float32)[None, :]
    growth = 1.0 + 2.0 * position / max(TOKENS - 1, 1)
    return (0.5 * normal_part * growth[:, :, None]).astype(jnp.bfloat16)


def block_scale(own_key, dims, split, least, largest):
    loudness = 1.0
    for dim, shards_of in split:
        draws = jax.random.uniform(jax.random.fold_in(jax.random.fold_in(own_key, 6), dim), (shards_of,), jnp.float32, least / len(split), largest / len(split))
        loudness = loudness * jnp.repeat(jnp.exp(draws), dims[dim] // shards_of).reshape((-1,) + (1,) * (len(dims) - 1 - dim))
    return loudness


def bell_draw(key, shape, width, limit, shards=(), kind=jnp.bfloat16):
    values = jax.random.normal(key, shape, jnp.float32) * width
    if len(shards) > 0:
        values = block_scale(key, shape, shards, -0.22, 0.18) * values
    return jnp.clip(values, min=-limit, max=limit).astype(kind)


def setup_inputs(seed: int = 0) -> dict:
    arg_keys = jax.random.split(jax.random.key(seed), 7)
    return {
        "queries": bell_draw(arg_keys[0], (VIEWS, LENGTH, D), 1.0, 6.0, ((0, 32), (1, 8))),
        "keys": bell_draw(arg_keys[1], (VIEWS, LENGTH, D), 1.0, 6.0, ((0, 32), (1, 8))),
        "values": bell_draw(arg_keys[2], (VIEWS, LENGTH, D), 1.0, 6.0, ((0, 32), (1, 8))),
        "query_gain": jnp.clip(jnp.exp(jax.random.uniform(arg_keys[3], (D,), jnp.float32, math.log(1.0), math.log(2.2))), 1.0, 2.2),
        "key_gain": jnp.clip(jnp.exp(jax.random.uniform(arg_keys[4], (D,), jnp.float32, math.log(1.0), math.log(2.2))), 1.0, 2.2),
        "cotangent": draw_cotangent(jax.random.fold_in(arg_keys[6], 71), 0),
    }


def contract_last(left, right):
    return lax.dot_general(left, right, (((1,), (1,)), ((), ())), preferred_element_type=jnp.float32)

def contract_first(left, right):
    return lax.dot_general(left, right, (((0,), (0,)), ((), ())), preferred_element_type=jnp.float32)

def layer_norm(entries, gain):
    centred = entries - lax.optimization_barrier(jnp.mean(entries, axis=-1, keepdims=True))
    inverse = lax.rsqrt(lax.optimization_barrier(jnp.mean(centred * centred, axis=-1, keepdims=True)) + 1e-06)
    normal_hat = centred * inverse
    return (normal_hat, inverse, (normal_hat * gain).astype(jnp.bfloat16))

def norm_back(normed_grad, normal_hat, inverse, gain):
    upstream = normed_grad.astype(jnp.float32)
    scaled = upstream * gain
    result = inverse * (scaled - lax.optimization_barrier(jnp.mean(scaled, axis=-1, keepdims=True)) - normal_hat * lax.optimization_barrier(jnp.mean(scaled * normal_hat, axis=-1, keepdims=True)))
    return (result.astype(jnp.bfloat16), lax.optimization_barrier(jnp.sum(upstream * normal_hat, axis=-2)))

def attend(query_normed, key_normed, head_values, upstream):
    factor = query_normed.shape[-1] ** (-0.5)
    scores = contract_last(query_normed, key_normed) * factor
    raised = jnp.exp(scores)
    weights = raised / lax.optimization_barrier(jnp.sum(raised, axis=-1, keepdims=True))
    weights_low = weights.astype(jnp.bfloat16)
    attended = jnp.dot(weights_low, head_values, preferred_element_type=jnp.float32).astype(jnp.bfloat16)
    value_grad = contract_first(weights_low, upstream).astype(jnp.bfloat16)
    weights_grad = contract_last(upstream, head_values)
    inner = lax.optimization_barrier(jnp.sum(weights * weights_grad, axis=-1, keepdims=True))
    score_grad = (weights * (weights_grad - inner)).astype(jnp.bfloat16)
    query_side = (jnp.dot(score_grad, key_normed, preferred_element_type=jnp.float32) * factor).astype(jnp.bfloat16)
    key_side = (contract_first(score_grad, query_normed) * factor).astype(jnp.bfloat16)
    return (attended, query_side, key_side, value_grad)

def reference(queries, keys, values, query_gain, key_gain, cotangent):
    gains_query = query_gain.reshape(HEADS, HD)
    gains_key = key_gain.reshape(HEADS, HD)

    def one_view(totals, view_data):
        query_view, key_view, value_view, upstream_view = view_data

        def one_head(head_id):
            column_start = (head_id * HD).astype(jnp.int32)
            query_part = lax.dynamic_slice_in_dim(query_view, column_start, HD, 1).astype(jnp.float32)
            key_part = lax.dynamic_slice_in_dim(key_view, column_start, HD, 1).astype(jnp.float32)
            value_part = lax.dynamic_slice_in_dim(value_view, column_start, HD, 1)
            upstream_part = lax.dynamic_slice_in_dim(upstream_view, column_start, HD, 1)
            gain_q = lax.dynamic_index_in_dim(gains_query, head_id, 0, keepdims=False)
            gain_k = lax.dynamic_index_in_dim(gains_key, head_id, 0, keepdims=False)
            query_hat, query_inv, query_normed = layer_norm(query_part, gain_q)
            key_hat, key_inv, key_normed = layer_norm(key_part, gain_k)
            attended, query_side, key_side, value_grad = attend(query_normed, key_normed, value_part, upstream_part)
            query_grad, query_term = norm_back(query_side, query_hat, query_inv, gain_q)
            key_grad, key_term = norm_back(key_side, key_hat, key_inv, gain_k)
            return (attended, query_grad, key_grad, value_grad, query_term, key_term)
        results = lax.map(one_head, jnp.arange(HEADS, dtype=jnp.int32))
        joined = tuple((piece.transpose(1, 0, 2).reshape(LENGTH, HEADS * HD) for piece in results[:4]))
        totals = (totals[0] + results[4].reshape(-1), totals[1] + results[5].reshape(-1))
        return (totals, joined)
    initial = (jnp.zeros((HEADS * HD,), jnp.float32), jnp.zeros((HEADS * HD,), jnp.float32))
    totals, stacked = lax.scan(one_view, initial, (queries, keys, values, cotangent))
    return (stacked[0], stacked[1], stacked[2], stacked[3], totals[0], totals[1])
```

```python
import functools

import jax
import jax.numpy as jnp
from jax import lax
from jax.experimental import pallas as pl
from jax.experimental.pallas import tpu as pltpu
from jax.sharding import PartitionSpec as P

HEADS = 48
HD = 128
ROWS = 8
MINE = HEADS // ROWS
TOK = 128
LENGTH = ROWS * TOK
WIDE = MINE * HD
BLK = 256
NEAR = 8
FAR = 4
ORDER = (4, 3, 5, 2, 6, 1, 7)
EARLY = 3
FACTOR = HD**-0.5
LOG2E = 1.4426950408889634
MESH = pl.DeviceIdType.MESH


def nn(left, right):
    return lax.dot_general(left, right, (((1,), (0,)), ((), ())), preferred_element_type=jnp.float32)


def nt(left, right):
    return lax.dot_general(left, right, (((1,), (1,)), ((), ())), preferred_element_type=jnp.float32)


def normalise(entries):
    centred = entries - jnp.mean(entries, axis=-1, keepdims=True)
    inverse = lax.rsqrt(jnp.mean(centred * centred, axis=-1, keepdims=True) + 1e-06)
    return centred * inverse, inverse


def norm_back(side, hat, inverse, gain):
    upstream = side.astype(jnp.float32)
    scaled = upstream * gain
    result = inverse * (
        scaled
        - jnp.mean(scaled, axis=-1, keepdims=True)
        - hat * jnp.mean(scaled * hat, axis=-1, keepdims=True)
    )
    return result.astype(jnp.bfloat16), jnp.sum(upstream * hat, axis=0, keepdims=True)


def drain(ref, sem):
    pltpu.make_async_copy(ref, ref, sem).wait()


def kernel(
    q_ref, k_ref, v_ref, g_ref, qgain_ref, kgain_ref,
    att_ref, dq_ref, dk_ref, dv_ref, gq_ref, gk_ref,
    land, res, qhat, khat, qinv, kinv, qn, kn, knt, vt, dk_acc, dv_acc,
    part, land1, sum1, land2, sum2, land3,
    f_send, f_recv, own_in, r_send, r_recv, own_out, g_send, g_recv,
):
    me = lax.axis_index("row")
    col = lax.axis_index("col")
    near = lax.rem(col, NEAR)
    far = lax.div(col, NEAR)
    sources = (q_ref, k_ref, v_ref, g_ref)
    targets = (att_ref, dq_ref, dk_ref, dv_ref)

    def row_peer(d):
        return lax.rem(me + d, ROWS)

    def near_peer(d):
        return far * NEAR + lax.rem(near + d, NEAR)

    def far_peer(d):
        return lax.rem(far + d, FAR) * NEAR + near

    barrier = pltpu.get_barrier_semaphore()
    for d in range(1, ROWS):
        pl.semaphore_signal(barrier, inc=1, device_id=(row_peer(d), col), device_id_type=MESH)
    for d in range(1, NEAR):
        pl.semaphore_signal(barrier, inc=1, device_id=(me, near_peer(d)), device_id_type=MESH)
    for d in range(1, FAR):
        pl.semaphore_signal(barrier, inc=1, device_id=(me, far_peer(d)), device_id_type=MESH)
    pl.semaphore_wait(barrier, ROWS + NEAR + FAR - 3)

    def columns(owner, h):
        return pl.ds(pl.multiple_of(owner * WIDE + h * HD, HD), HD)

    def rows(owner):
        return pl.ds(pl.multiple_of(owner * TOK, TOK), TOK)

    def send_forward(h, carry):
        for d in ORDER:
            peer = row_peer(d)
            for t in range(4):
                pltpu.make_async_remote_copy(
                    src_ref=sources[t].at[0, :, columns(peer, h)],
                    dst_ref=land.at[h, t, rows(me), :],
                    send_sem=f_send,
                    recv_sem=f_recv.at[h],
                    device_id=(peer, col),
                    device_id_type=MESH,
                ).start()
        for t in range(4):
            pltpu.make_async_copy(
                sources[t].at[0, :, columns(me, h)], land.at[h, t, rows(me), :], own_in.at[h]
            ).start()
        return carry

    lax.fori_loop(0, MINE, send_forward, 0)

    def send_back(h):
        for d in ORDER:
            peer = row_peer(d)
            for t in range(4):
                pltpu.make_async_remote_copy(
                    src_ref=res.at[h, t, rows(peer), :],
                    dst_ref=targets[t].at[0, :, columns(me, h)],
                    send_sem=r_send,
                    recv_sem=r_recv.at[t],
                    device_id=(peer, col),
                    device_id_type=MESH,
                ).start()
        for t in range(4):
            pltpu.make_async_copy(
                res.at[h, t, rows(me), :], targets[t].at[0, :, columns(me, h)], own_out
            ).start()

    part[...] = jnp.zeros_like(part)

    def one_head(h, carry):
        drain(land.at[h, :, pl.ds(0, LENGTH - TOK), :], f_recv.at[h])
        drain(land.at[h, :, pl.ds(0, TOK), :], own_in.at[h])
        gain_q = qgain_ref[pl.ds(me * MINE + h, 1), :]
        gain_k = kgain_ref[pl.ds(me * MINE + h, 1), :]
        hat, inverse = normalise(land[h, 0].astype(jnp.float32))
        qhat[...] = hat
        qinv[...] = inverse
        qn[...] = (hat * gain_q).astype(jnp.bfloat16)
        hat, inverse = normalise(land[h, 1].astype(jnp.float32))
        khat[...] = hat
        kinv[...] = inverse
        normed = hat * gain_k
        kn[...] = normed.astype(jnp.bfloat16)
        knt[...] = normed.T.astype(jnp.bfloat16)
        vt[...] = land[h, 2].astype(jnp.float32).T.astype(jnp.bfloat16)
        dk_acc[...] = jnp.zeros_like(dk_acc)
        dv_acc[...] = jnp.zeros_like(dv_acc)

        def block(b, total):
            mine = pl.ds(pl.multiple_of(b * BLK, BLK), BLK)
            q_blk = qn[mine, :]
            g_blk = land[h, 3, mine, :]
            raised = jnp.exp2(nt(kn[...], q_blk) * (FACTOR * LOG2E))
            weights = raised * (1.0 / jnp.sum(raised, axis=0, keepdims=True))
            low = weights.astype(jnp.bfloat16)
            res[h, 0, mine, :] = nn(vt[...], low).T.astype(jnp.bfloat16)
            dv_acc[...] += nn(low, g_blk)
            weights_grad = nt(land[h, 2], g_blk)
            inner = jnp.sum(weights * weights_grad, axis=0, keepdims=True)
            score_grad = (weights * (weights_grad - inner)).astype(jnp.bfloat16)
            dk_acc[...] += nn(score_grad, q_blk)
            side = (nn(knt[...], score_grad) * FACTOR).T.astype(jnp.bfloat16)
            grad, term = norm_back(side, qhat[mine, :], qinv[mine, :], gain_q)
            res[h, 1, mine, :] = grad
            return total + term

        total_q = lax.fori_loop(0, LENGTH // BLK, block, jnp.zeros((1, HD), jnp.float32))
        res[h, 3] = dv_acc[...].astype(jnp.bfloat16)
        side = (dk_acc[...] * FACTOR).astype(jnp.bfloat16)
        grad, total_k = norm_back(side, khat[...], kinv[...], gain_k)
        res[h, 2] = grad
        part[pl.ds(h, 1), :] = total_q
        part[pl.ds(8 + h, 1), :] = total_k

        @pl.when(h < EARLY)
        def _():
            send_back(h)

        return carry

    lax.fori_loop(0, MINE, one_head, 0)

    def share(stage, source, slots, slot, peers):
        for device in peers:
            pltpu.make_async_remote_copy(
                src_ref=source,
                dst_ref=slots.at[slot],
                send_sem=g_send.at[stage],
                recv_sem=g_recv.at[stage],
                device_id=device,
                device_id_type=MESH,
            ).start()
        slots[slot] = source[...]

    def shared(stage, slots, count):
        drain(slots.at[pl.ds(0, count - 1)], g_recv.at[stage])

    share(0, part, land1, near, [(me, near_peer(d)) for d in range(1, NEAR)])
    send_back(3)
    shared(0, land1, NEAR)
    sum1[...] = jnp.sum(land1[...], axis=0)
    share(1, sum1, land2, far, [(me, far_peer(d)) for d in range(1, FAR)])
    send_back(4)
    shared(1, land2, FAR)
    sum2[...] = jnp.sum(land2[...], axis=0)
    share(2, sum2, land3, me, [(row_peer(d), col) for d in range(1, ROWS)])
    send_back(5)
    shared(2, land3, ROWS)
    for r in range(ROWS):
        gq_ref[r * MINE : (r + 1) * MINE, :] = land3[r, 0:MINE, :]
        gk_ref[r * MINE : (r + 1) * MINE, :] = land3[r, 8 : 8 + MINE, :]
    drain(land1.at[pl.ds(0, NEAR - 1)], g_send.at[0])
    drain(land2.at[pl.ds(0, FAR - 1)], g_send.at[1])
    drain(land3.at[pl.ds(0, ROWS - 1)], g_send.at[2])
    drain(land.at[:, :, pl.ds(0, LENGTH - TOK), :], f_send)
    drain(res.at[:, :, pl.ds(0, LENGTH - TOK), :], r_send)
    drain(res.at[:, :, pl.ds(0, TOK), :], own_out)
    for t in range(4):
        drain(targets[t].at[0, :, pl.ds(0, HEADS * HD - WIDE)], r_recv.at[t])


def body(queries, keys, values, query_gain, key_gain, cotangent):
    big = jax.ShapeDtypeStruct(queries.shape, jnp.bfloat16)
    small = jax.ShapeDtypeStruct((HEADS, HD), jnp.float32)
    hbm = pl.BlockSpec(memory_space=pl.ANY)
    vmem = pl.BlockSpec(memory_space=pltpu.VMEM)
    token_f32 = pltpu.VMEM((LENGTH, HD), jnp.float32)
    token_bf16 = pltpu.VMEM((LENGTH, HD), jnp.bfloat16)
    column = pltpu.VMEM((LENGTH, 1), jnp.float32)
    turned = pltpu.VMEM((HD, LENGTH), jnp.bfloat16)
    blocks = pltpu.VMEM((MINE, 4, LENGTH, HD), jnp.bfloat16)
    dma = pltpu.SemaphoreType.DMA
    attended, query_grad, key_grad, value_grad, query_total, key_total = pl.pallas_call(
        kernel,
        out_shape=(big, big, big, big, small, small),
        in_specs=[hbm] * 4 + [vmem] * 2,
        out_specs=(hbm, hbm, hbm, hbm, vmem, vmem),
        scratch_shapes=[
            blocks, blocks, token_f32, token_f32, column, column, token_bf16, token_bf16,
            turned, turned, token_f32, token_f32,
            pltpu.VMEM((16, HD), jnp.float32),
            pltpu.VMEM((NEAR, 16, HD), jnp.float32),
            pltpu.VMEM((16, HD), jnp.float32),
            pltpu.VMEM((FAR, 16, HD), jnp.float32),
            pltpu.VMEM((16, HD), jnp.float32),
            pltpu.VMEM((ROWS, 16, HD), jnp.float32),
            dma, dma((MINE,)), dma((MINE,)), dma, dma((4,)), dma, dma((3,)), dma((3,)),
        ],
        compiler_params=pltpu.CompilerParams(
            collective_id=0, has_side_effects=True, vmem_limit_bytes=56 * 2**20
        ),
        cost_estimate=pl.CostEstimate(
            flops=12 * MINE * LENGTH * LENGTH * HD,
            bytes_accessed=16 * TOK * HEADS * HD,
            transcendentals=MINE * LENGTH * LENGTH,
        ),
        name="attention_exchange",
    )(
        queries, keys, values, cotangent,
        query_gain.reshape(HEADS, HD), key_gain.reshape(HEADS, HD),
    )
    return (
        attended, query_grad, key_grad, value_grad,
        query_total.reshape(-1), key_total.reshape(-1),
    )


def solution(mesh):
    return jax.shard_map(
        body,
        mesh=mesh,
        in_specs=(
            P("col", "row", None),
            P("col", "row", None),
            P("col", "row", None),
            P(),
            P(),
            P("col", "row", None),
        ),
        out_specs=(
            P("col", "row", None),
            P("col", "row", None),
            P("col", "row", None),
            P("col", "row", None),
            P(),
            P(),
        ),
        check_vma=False,
    )
```

```python
import functools

import jax
import jax.numpy as jnp
from jax import lax
from jax.experimental import pallas as pl
from jax.experimental.pallas import tpu as pltpu
from jax.sharding import PartitionSpec as P

HEADS = 48
HD = 128
ROWS = 8
MINE = HEADS // ROWS
TOK = 128
LENGTH = ROWS * TOK
WIDE = MINE * HD
BLK = 256
NEAR = 8
FAR = 4
ORDER = (4, 3, 5, 2, 6, 1, 7)
EARLY = 3
FACTOR = HD**-0.5
LOG2E = 1.4426950408889634
MESH = pl.DeviceIdType.MESH


def nn(left, right):
    return lax.dot_general(left, right, (((1,), (0,)), ((), ())), preferred_element_type=jnp.float32)


def nt(left, right):
    return lax.dot_general(left, right, (((1,), (1,)), ((), ())), preferred_element_type=jnp.float32)


def normalise(entries):
    centred = entries - jnp.mean(entries, axis=-1, keepdims=True)
    inverse = lax.rsqrt(jnp.mean(centred * centred, axis=-1, keepdims=True) + 1e-06)
    return centred * inverse, inverse


def norm_back(side, hat, inverse, gain):
    upstream = side.astype(jnp.float32)
    scaled = upstream * gain
    result = inverse * (
        scaled
        - jnp.mean(scaled, axis=-1, keepdims=True)
        - hat * jnp.mean(scaled * hat, axis=-1, keepdims=True)
    )
    return result.astype(jnp.bfloat16), jnp.sum(upstream * hat, axis=0, keepdims=True)


def drain(ref, sem):
    pltpu.make_async_copy(ref, ref, sem).wait()


def kernel(
    q_ref, k_ref, v_ref, g_ref, qgain_hbm, kgain_hbm,
    att_ref, dq_ref, dk_ref, dv_ref, gq_ref, gk_ref,
    land, res, qhat, khat, qinv, kinv, qn, kn, knt, vt, dk_acc, dv_acc,
    part, land1, sum1, land2, sum2, land3, total_q, total_k, qgain_ref, kgain_ref,
    f_send, f_recv, own_in, r_send, r_recv, own_out, g_send, g_recv, g_out, g_in,
):
    me = lax.axis_index("row")
    col = lax.axis_index("col")
    near = lax.rem(col, NEAR)
    far = lax.div(col, NEAR)
    sources = (q_ref, k_ref, v_ref, g_ref)
    targets = (att_ref, dq_ref, dk_ref, dv_ref)

    def row_peer(d):
        return lax.rem(me + d, ROWS)

    def near_peer(d):
        return far * NEAR + lax.rem(near + d, NEAR)

    def far_peer(d):
        return lax.rem(far + d, FAR) * NEAR + near

    pltpu.make_async_copy(qgain_hbm, qgain_ref, g_in.at[0]).start()
    pltpu.make_async_copy(kgain_hbm, kgain_ref, g_in.at[1]).start()

    barrier = pltpu.get_barrier_semaphore()
    for d in range(1, ROWS):
        pl.semaphore_signal(barrier, inc=1, device_id=(row_peer(d), col), device_id_type=MESH)
    for d in range(1, NEAR):
        pl.semaphore_signal(barrier, inc=1, device_id=(me, near_peer(d)), device_id_type=MESH)
    for d in range(1, FAR):
        pl.semaphore_signal(barrier, inc=1, device_id=(me, far_peer(d)), device_id_type=MESH)
    pl.semaphore_wait(barrier, ROWS + NEAR + FAR - 3)

    def columns(owner, h):
        return pl.ds(pl.multiple_of(owner * WIDE + h * HD, HD), HD)

    def rows(owner):
        return pl.ds(pl.multiple_of(owner * TOK, TOK), TOK)

    def send_forward(h, carry):
        for d in ORDER:
            peer = row_peer(d)
            for t in range(4):
                pltpu.make_async_remote_copy(
                    src_ref=sources[t].at[0, :, columns(peer, h)],
                    dst_ref=land.at[h, t, rows(me), :],
                    send_sem=f_send,
                    recv_sem=f_recv.at[h],
                    device_id=(peer, col),
                    device_id_type=MESH,
                ).start()
        for t in range(4):
            pltpu.make_async_copy(
                sources[t].at[0, :, columns(me, h)], land.at[h, t, rows(me), :], own_in.at[h]
            ).start()
        return carry

    lax.fori_loop(0, MINE, send_forward, 0)

    def send_back(h):
        for d in ORDER:
            peer = row_peer(d)
            for t in range(4):
                pltpu.make_async_remote_copy(
                    src_ref=res.at[h, t, rows(peer), :],
                    dst_ref=targets[t].at[0, :, columns(me, h)],
                    send_sem=r_send,
                    recv_sem=r_recv.at[t],
                    device_id=(peer, col),
                    device_id_type=MESH,
                ).start()
        for t in range(4):
            pltpu.make_async_copy(
                res.at[h, t, rows(me), :], targets[t].at[0, :, columns(me, h)], own_out
            ).start()

    part[...] = jnp.zeros_like(part)
    drain(qgain_ref, g_in.at[0])
    drain(kgain_ref, g_in.at[1])

    def one_head(h, carry):
        drain(land.at[h, :, pl.ds(0, LENGTH - TOK), :], f_recv.at[h])
        drain(land.at[h, :, pl.ds(0, TOK), :], own_in.at[h])
        gain_q = qgain_ref[pl.ds(me * MINE + h, 1), :]
        gain_k = kgain_ref[pl.ds(me * MINE + h, 1), :]
        hat, inverse = normalise(land[h, 0].astype(jnp.float32))
        qhat[...] = hat
        qinv[...] = inverse
        qn[...] = (hat * gain_q).astype(jnp.bfloat16)
        hat, inverse = normalise(land[h, 1].astype(jnp.float32))
        khat[...] = hat
        kinv[...] = inverse
        normed = hat * gain_k
        kn[...] = normed.astype(jnp.bfloat16)
        knt[...] = normed.T.astype(jnp.bfloat16)
        vt[...] = land[h, 2].astype(jnp.float32).T.astype(jnp.bfloat16)
        dk_acc[...] = jnp.zeros_like(dk_acc)
        dv_acc[...] = jnp.zeros_like(dv_acc)

        def block(b, total):
            mine = pl.ds(pl.multiple_of(b * BLK, BLK), BLK)
            q_blk = qn[mine, :]
            g_blk = land[h, 3, mine, :]
            raised = jnp.exp2(nt(kn[...], q_blk) * (FACTOR * LOG2E))
            weights = raised * (1.0 / jnp.sum(raised, axis=0, keepdims=True))
            low = weights.astype(jnp.bfloat16)
            res[h, 0, mine, :] = nn(vt[...], low).T.astype(jnp.bfloat16)
            dv_acc[...] += nn(low, g_blk)
            weights_grad = nt(land[h, 2], g_blk)
            inner = jnp.sum(weights * weights_grad, axis=0, keepdims=True)
            score_grad = (weights * (weights_grad - inner)).astype(jnp.bfloat16)
            dk_acc[...] += nn(score_grad, q_blk)
            side = (nn(knt[...], score_grad) * FACTOR).T.astype(jnp.bfloat16)
            grad, term = norm_back(side, qhat[mine, :], qinv[mine, :], gain_q)
            res[h, 1, mine, :] = grad
            return total + term

        sum_q = lax.fori_loop(0, LENGTH // BLK, block, jnp.zeros((1, HD), jnp.float32))
        res[h, 3] = dv_acc[...].astype(jnp.bfloat16)
        side = (dk_acc[...] * FACTOR).astype(jnp.bfloat16)
        grad, sum_k = norm_back(side, khat[...], kinv[...], gain_k)
        res[h, 2] = grad
        part[pl.ds(h, 1), :] = sum_q
        part[pl.ds(8 + h, 1), :] = sum_k

        @pl.when(h < EARLY)
        def _():
            send_back(h)

        return carry

    lax.fori_loop(0, MINE, one_head, 0)

    def share(stage, source, slots, slot, peers):
        for device in peers:
            pltpu.make_async_remote_copy(
                src_ref=source,
                dst_ref=slots.at[slot],
                send_sem=g_send.at[stage],
                recv_sem=g_recv.at[stage],
                device_id=device,
                device_id_type=MESH,
            ).start()
        slots[slot] = source[...]

    def shared(stage, slots, count):
        drain(slots.at[pl.ds(0, count - 1)], g_recv.at[stage])

    share(0, part, land1, near, [(me, near_peer(d)) for d in range(1, NEAR)])
    send_back(3)
    shared(0, land1, NEAR)
    sum1[...] = jnp.sum(land1[...], axis=0)
    share(1, sum1, land2, far, [(me, far_peer(d)) for d in range(1, FAR)])
    send_back(4)
    shared(1, land2, FAR)
    sum2[...] = jnp.sum(land2[...], axis=0)
    share(2, sum2, land3, me, [(row_peer(d), col) for d in range(1, ROWS)])
    send_back(5)
    shared(2, land3, ROWS)
    for r in range(ROWS):
        total_q[r * MINE : (r + 1) * MINE, :] = land3[r, 0:MINE, :]
        total_k[r * MINE : (r + 1) * MINE, :] = land3[r, 8 : 8 + MINE, :]
    pltpu.make_async_copy(total_q, gq_ref, g_out.at[0]).start()
    pltpu.make_async_copy(total_k, gk_ref, g_out.at[1]).start()
    drain(total_q, g_out.at[0])
    drain(total_k, g_out.at[1])
    drain(land1.at[pl.ds(0, NEAR - 1)], g_send.at[0])
    drain(land2.at[pl.ds(0, FAR - 1)], g_send.at[1])
    drain(land3.at[pl.ds(0, ROWS - 1)], g_send.at[2])
    drain(land.at[:, :, pl.ds(0, LENGTH - TOK), :], f_send)
    drain(res.at[:, :, pl.ds(0, LENGTH - TOK), :], r_send)
    drain(res.at[:, :, pl.ds(0, TOK), :], own_out)
    for t in range(4):
        drain(targets[t].at[0, :, pl.ds(0, HEADS * HD - WIDE)], r_recv.at[t])


def settle(*refs):
    sems = refs[-1]
    count = len(refs) // 2
    copies = [
        pltpu.make_async_copy(refs[i], refs[count + i], sems.at[i]) for i in range(count)
    ]
    for copy in copies:
        copy.start()
    for copy in copies:
        copy.wait()


def body(queries, keys, values, query_gain, key_gain, cotangent):
    big = jax.ShapeDtypeStruct(queries.shape, jnp.bfloat16)
    small = jax.ShapeDtypeStruct((HEADS, HD), jnp.float32)
    hbm = pl.BlockSpec(memory_space=pl.ANY)
    token_f32 = pltpu.VMEM((LENGTH, HD), jnp.float32)
    token_bf16 = pltpu.VMEM((LENGTH, HD), jnp.bfloat16)
    column = pltpu.VMEM((LENGTH, 1), jnp.float32)
    turned = pltpu.VMEM((HD, LENGTH), jnp.bfloat16)
    blocks = pltpu.VMEM((MINE, 4, LENGTH, HD), jnp.bfloat16)
    dma = pltpu.SemaphoreType.DMA
    held = pltpu.VMEM(queries.shape, jnp.bfloat16)
    held_small = pltpu.VMEM((HEADS, HD), jnp.float32)
    results = pl.pallas_call(
        kernel,
        out_shape=(held, held, held, held, held_small, held_small),
        in_specs=[hbm] * 6,
        out_specs=(hbm,) * 6,
        scratch_shapes=[
            blocks, blocks, token_f32, token_f32, column, column, token_bf16, token_bf16,
            turned, turned, token_f32, token_f32,
            pltpu.VMEM((16, HD), jnp.float32),
            pltpu.VMEM((NEAR, 16, HD), jnp.float32),
            pltpu.VMEM((16, HD), jnp.float32),
            pltpu.VMEM((FAR, 16, HD), jnp.float32),
            pltpu.VMEM((16, HD), jnp.float32),
            pltpu.VMEM((ROWS, 16, HD), jnp.float32),
            pltpu.VMEM((HEADS, HD), jnp.float32),
            pltpu.VMEM((HEADS, HD), jnp.float32),
            pltpu.VMEM((HEADS, HD), jnp.float32),
            pltpu.VMEM((HEADS, HD), jnp.float32),
            dma, dma((MINE,)), dma((MINE,)), dma, dma((4,)), dma, dma((3,)), dma((3,)), dma((2,)), dma((2,)),
        ],
        compiler_params=pltpu.CompilerParams(
            collective_id=0, has_side_effects=True, vmem_limit_bytes=40 * 2**20
        ),
        cost_estimate=pl.CostEstimate(
            flops=12 * MINE * LENGTH * LENGTH * HD,
            bytes_accessed=16 * TOK * HEADS * HD,
            transcendentals=MINE * LENGTH * LENGTH,
        ),
        name="attention_exchange",
    )(
        *(
            pltpu.with_memory_space_constraint(operand, pltpu.HBM)
            for operand in (
                queries, keys, values, cotangent,
                query_gain.reshape(HEADS, HD), key_gain.reshape(HEADS, HD),
            )
        )
    )
    attended, query_grad, key_grad, value_grad, query_total, key_total = pl.pallas_call(
        settle,
        out_shape=(big, big, big, big, small, small),
        in_specs=[hbm] * 6,
        out_specs=(hbm,) * 6,
        scratch_shapes=[dma((6,))],
        compiler_params=pltpu.CompilerParams(vmem_limit_bytes=2**20),
        name="settle",
    )(*(pltpu.with_memory_space_constraint(result, pltpu.VMEM) for result in results))
    return (
        attended, query_grad, key_grad, value_grad,
        query_total.reshape(-1), key_total.reshape(-1),
    )


def solution(mesh):
    return jax.shard_map(
        body,
        mesh=mesh,
        in_specs=(
            P("col", "row", None),
            P("col", "row", None),
            P("col", "row", None),
            P(),
            P(),
            P("col", "row", None),
        ),
        out_specs=(
            P("col", "row", None),
            P("col", "row", None),
            P("col", "row", None),
            P("col", "row", None),
            P(),
            P(),
        ),
        check_vma=False,
    )
```

```python
import functools

import jax
import jax.numpy as jnp
from jax import lax
from jax.experimental import pallas as pl
from jax.experimental.pallas import tpu as pltpu
from jax.sharding import PartitionSpec as P

HEADS = 48
HD = 128
ROWS = 8
MINE = HEADS // ROWS
TOK = 128
LENGTH = ROWS * TOK
WIDE = MINE * HD
BLK = 256
NEAR = 8
FAR = 4
ORDER = (4, 3, 5, 2, 6, 1, 7)
EARLY = 2
FACTOR = HD**-0.5
LOG2E = 1.4426950408889634
MESH = pl.DeviceIdType.MESH


def nn(left, right):
    return lax.dot_general(left, right, (((1,), (0,)), ((), ())), preferred_element_type=jnp.float32)


def nt(left, right):
    return lax.dot_general(left, right, (((1,), (1,)), ((), ())), preferred_element_type=jnp.float32)


def normalise(entries):
    centred = entries - jnp.mean(entries, axis=-1, keepdims=True)
    inverse = lax.rsqrt(jnp.mean(centred * centred, axis=-1, keepdims=True) + 1e-06)
    return centred * inverse, inverse


def norm_back(side, hat, inverse, gain):
    upstream = side.astype(jnp.float32)
    scaled = upstream * gain
    result = inverse * (
        scaled
        - jnp.mean(scaled, axis=-1, keepdims=True)
        - hat * jnp.mean(scaled * hat, axis=-1, keepdims=True)
    )
    return result.astype(jnp.bfloat16), jnp.sum(upstream * hat, axis=0, keepdims=True)


def drain(ref, sem):
    pltpu.make_async_copy(ref, ref, sem).wait()


def kernel(
    q_ref, k_ref, v_ref, g_ref, qgain_hbm, kgain_hbm,
    att_ref, dq_ref, dk_ref, dv_ref, gq_ref, gk_ref,
    land, res, qhat, khat, qinv, kinv, qn, kn, knt, vt, dk_acc, dv_acc,
    part, land1, sum1, land2, sum2, land3, land4, total_q, total_k, qgain_ref, kgain_ref,
    f_send, f_recv, own_in, r_send, r_recv, own_out, g_send, g_recv, g_out, g_in, rings_here,
):
    me = lax.axis_index("row")
    col = lax.axis_index("col")
    near = lax.rem(col, NEAR)
    far = lax.div(col, NEAR)
    sources = (q_ref, k_ref, v_ref, g_ref)
    targets = (att_ref, dq_ref, dk_ref, dv_ref)

    def row_peer(d):
        return lax.rem(me + d, ROWS)

    def near_peer(d):
        return far * NEAR + lax.rem(near + d, NEAR)

    def far_peer(d):
        return lax.rem(far + d, FAR) * NEAR + near

    pltpu.make_async_copy(qgain_hbm, qgain_ref, g_in.at[0]).start()
    pltpu.make_async_copy(kgain_hbm, kgain_ref, g_in.at[1]).start()

    barrier = pltpu.get_barrier_semaphore()
    for d in range(1, ROWS):
        pl.semaphore_signal(barrier, inc=1, device_id=(row_peer(d), col), device_id_type=MESH)
    plane_peers = [(me, near_peer(d)) for d in range(1, NEAR)]
    plane_peers += [(me, far_peer(d)) for d in range(1, FAR)]

    @pl.when(me == 0)
    def _():
        for device in plane_peers:
            pl.semaphore_signal(barrier, inc=1, device_id=device, device_id_type=MESH)
        pl.semaphore_wait(barrier, ROWS - 1 + len(plane_peers))
        for device in plane_peers:
            pl.semaphore_signal(rings_here, inc=1, device_id=device, device_id_type=MESH)

    @pl.when(me != 0)
    def _():
        pl.semaphore_wait(barrier, ROWS - 1)

    def columns(owner, h):
        return pl.ds(pl.multiple_of(owner * WIDE + h * HD, HD), HD)

    def rows(owner):
        return pl.ds(pl.multiple_of(owner * TOK, TOK), TOK)

    def send_forward(h, carry):
        for d in ORDER:
            peer = row_peer(d)
            for t in range(4):
                pltpu.make_async_remote_copy(
                    src_ref=sources[t].at[0, :, columns(peer, h)],
                    dst_ref=land.at[h, t, rows(me), :],
                    send_sem=f_send,
                    recv_sem=f_recv.at[h],
                    device_id=(peer, col),
                    device_id_type=MESH,
                ).start()
        for t in range(4):
            pltpu.make_async_copy(
                sources[t].at[0, :, columns(me, h)], land.at[h, t, rows(me), :], own_in.at[h]
            ).start()
        return carry

    lax.fori_loop(0, MINE, send_forward, 0)

    def send_back(h):
        for d in ORDER:
            peer = row_peer(d)
            for t in range(4):
                pltpu.make_async_remote_copy(
                    src_ref=res.at[h, t, rows(peer), :],
                    dst_ref=targets[t].at[0, :, columns(me, h)],
                    send_sem=r_send,
                    recv_sem=r_recv.at[t],
                    device_id=(peer, col),
                    device_id_type=MESH,
                ).start()
        for t in range(4):
            pltpu.make_async_copy(
                res.at[h, t, rows(me), :], targets[t].at[0, :, columns(me, h)], own_out
            ).start()

    part[...] = jnp.zeros_like(part)
    drain(qgain_ref, g_in.at[0])
    drain(kgain_ref, g_in.at[1])

    def one_head(h, carry):
        drain(land.at[h, :, pl.ds(0, LENGTH - TOK), :], f_recv.at[h])
        drain(land.at[h, :, pl.ds(0, TOK), :], own_in.at[h])
        gain_q = qgain_ref[pl.ds(me * MINE + h, 1), :]
        gain_k = kgain_ref[pl.ds(me * MINE + h, 1), :]
        hat, inverse = normalise(land[h, 0].astype(jnp.float32))
        qhat[...] = hat
        qinv[...] = inverse
        qn[...] = (hat * gain_q).astype(jnp.bfloat16)
        hat, inverse = normalise(land[h, 1].astype(jnp.float32))
        khat[...] = hat
        kinv[...] = inverse
        normed = hat * gain_k
        kn[...] = normed.astype(jnp.bfloat16)
        knt[...] = normed.T.astype(jnp.bfloat16)
        vt[...] = land[h, 2].astype(jnp.float32).T.astype(jnp.bfloat16)
        dk_acc[...] = jnp.zeros_like(dk_acc)
        dv_acc[...] = jnp.zeros_like(dv_acc)

        def block(b, total):
            mine = pl.ds(pl.multiple_of(b * BLK, BLK), BLK)
            q_blk = qn[mine, :]
            g_blk = land[h, 3, mine, :]
            raised = jnp.exp2(nt(kn[...], q_blk) * (FACTOR * LOG2E))
            weights = raised * (1.0 / jnp.sum(raised, axis=0, keepdims=True))
            low = weights.astype(jnp.bfloat16)
            res[h, 0, mine, :] = nn(vt[...], low).T.astype(jnp.bfloat16)
            dv_acc[...] += nn(low, g_blk)
            weights_grad = nt(land[h, 2], g_blk)
            inner = jnp.sum(weights * weights_grad, axis=0, keepdims=True)
            score_grad = (weights * (weights_grad - inner)).astype(jnp.bfloat16)
            dk_acc[...] += nn(score_grad, q_blk)
            side = (nn(knt[...], score_grad) * FACTOR).T.astype(jnp.bfloat16)
            grad, term = norm_back(side, qhat[mine, :], qinv[mine, :], gain_q)
            res[h, 1, mine, :] = grad
            return total + term

        sum_q = lax.fori_loop(0, LENGTH // BLK, block, jnp.zeros((1, HD), jnp.float32))
        res[h, 3] = dv_acc[...].astype(jnp.bfloat16)
        side = (dk_acc[...] * FACTOR).astype(jnp.bfloat16)
        grad, sum_k = norm_back(side, khat[...], kinv[...], gain_k)
        res[h, 2] = grad
        part[lax.div(h, 2), pl.ds(lax.rem(h, 2), 1), :] = sum_q
        part[MINE // 2 + lax.div(h, 2), pl.ds(lax.rem(h, 2), 1), :] = sum_k

        @pl.when(h < EARLY)
        def _():
            send_back(h)

        return carry

    lax.fori_loop(0, MINE, one_head, 0)

    @pl.when(me == 0)
    def _():
        pl.semaphore_wait(rings_here, len(plane_peers))
        for d in range(1, ROWS):
            pl.semaphore_signal(rings_here, inc=1, device_id=(row_peer(d), col), device_id_type=MESH)

    @pl.when(me != 0)
    def _():
        pl.semaphore_wait(rings_here, 1)

    def share(stage, source, slots, slot, device):
        pltpu.make_async_remote_copy(
            src_ref=source,
            dst_ref=slots.at[slot],
            send_sem=g_send.at[stage],
            recv_sem=g_recv.at[stage],
            device_id=device,
            device_id_type=MESH,
        ).start()

    def shared(stage, slots, count):
        drain(slots.at[pl.ds(0, count - 1)], g_recv.at[stage])

    for d in range(1, NEAR):
        share(0, part.at[lax.rem(near + d, NEAR)], land1, near, (me, near_peer(d)))
    land1[near] = part[near]
    send_back(2)
    shared(0, land1, NEAR)
    sum1[...] = jnp.sum(land1[...], axis=0)
    for d in range(1, FAR):
        share(1, sum1, land2, far, (me, far_peer(d)))
    land2[far] = sum1[...]
    send_back(3)
    shared(1, land2, FAR)
    sum2[...] = jnp.sum(land2[...], axis=0)
    for d in range(1, ROWS):
        share(2, sum2, land3, me, (row_peer(d), col))
    land3[me] = sum2[...]
    send_back(4)
    shared(2, land3, ROWS)
    for d in range(1, NEAR):
        share(3, land3, land4, near, (me, near_peer(d)))
    land4[near] = land3[...]
    send_back(5)
    shared(3, land4, NEAR)
    for r in range(ROWS):
        for h in range(0, MINE, 2):
            total_q[r * MINE + h : r * MINE + h + 2, :] = land4[h // 2, r]
            total_k[r * MINE + h : r * MINE + h + 2, :] = land4[(MINE + h) // 2, r]
    pltpu.make_async_copy(total_q, gq_ref, g_out.at[0]).start()
    pltpu.make_async_copy(total_k, gk_ref, g_out.at[1]).start()
    drain(total_q, g_out.at[0])
    drain(total_k, g_out.at[1])
    drain(land1.at[pl.ds(0, NEAR - 1)], g_send.at[0])
    drain(land2.at[pl.ds(0, FAR - 1)], g_send.at[1])
    drain(land3.at[pl.ds(0, ROWS - 1)], g_send.at[2])
    drain(land4.at[pl.ds(0, NEAR - 1)], g_send.at[3])
    drain(land.at[:, :, pl.ds(0, LENGTH - TOK), :], f_send)
    drain(res.at[:, :, pl.ds(0, LENGTH - TOK), :], r_send)
    drain(res.at[:, :, pl.ds(0, TOK), :], own_out)
    for t in range(4):
        drain(targets[t].at[0, :, pl.ds(0, HEADS * HD - WIDE)], r_recv.at[t])


def settle(*refs):
    sems = refs[-1]
    count = len(refs) // 2
    copies = [
        pltpu.make_async_copy(refs[i], refs[count + i], sems.at[i]) for i in range(count)
    ]
    for copy in copies:
        copy.start()
    for copy in copies:
        copy.wait()


def body(queries, keys, values, query_gain, key_gain, cotangent):
    big = jax.ShapeDtypeStruct(queries.shape, jnp.bfloat16)
    small = jax.ShapeDtypeStruct((HEADS, HD), jnp.float32)
    hbm = pl.BlockSpec(memory_space=pl.ANY)
    token_f32 = pltpu.VMEM((LENGTH, HD), jnp.float32)
    token_bf16 = pltpu.VMEM((LENGTH, HD), jnp.bfloat16)
    column = pltpu.VMEM((LENGTH, 1), jnp.float32)
    turned = pltpu.VMEM((HD, LENGTH), jnp.bfloat16)
    blocks = pltpu.VMEM((MINE, 4, LENGTH, HD), jnp.bfloat16)
    dma = pltpu.SemaphoreType.DMA
    held = pltpu.VMEM(queries.shape, jnp.bfloat16)
    held_small = pltpu.VMEM((HEADS, HD), jnp.float32)
    results = pl.pallas_call(
        kernel,
        out_shape=(held, held, held, held, held_small, held_small),
        in_specs=[hbm] * 6,
        out_specs=(hbm,) * 6,
        scratch_shapes=[
            blocks, blocks, token_f32, token_f32, column, column, token_bf16, token_bf16,
            turned, turned, token_f32, token_f32,
            pltpu.VMEM((NEAR, 2, HD), jnp.float32),
            pltpu.VMEM((NEAR, 2, HD), jnp.float32),
            pltpu.VMEM((2, HD), jnp.float32),
            pltpu.VMEM((FAR, 2, HD), jnp.float32),
            pltpu.VMEM((2, HD), jnp.float32),
            pltpu.VMEM((ROWS, 2, HD), jnp.float32),
            pltpu.VMEM((NEAR, ROWS, 2, HD), jnp.float32),
            pltpu.VMEM((HEADS, HD), jnp.float32),
            pltpu.VMEM((HEADS, HD), jnp.float32),
            pltpu.VMEM((HEADS, HD), jnp.float32),
            pltpu.VMEM((HEADS, HD), jnp.float32),
            dma, dma((MINE,)), dma((MINE,)), dma, dma((4,)), dma, dma((4,)), dma((4,)), dma((2,)), dma((2,)),
            pltpu.SemaphoreType.REGULAR,
        ],
        compiler_params=pltpu.CompilerParams(
            collective_id=0, has_side_effects=True, vmem_limit_bytes=40 * 2**20
        ),
        cost_estimate=pl.CostEstimate(
            flops=12 * MINE * LENGTH * LENGTH * HD,
            bytes_accessed=16 * TOK * HEADS * HD,
            transcendentals=MINE * LENGTH * LENGTH,
        ),
        name="attention_exchange",
    )(
        *(
            pltpu.with_memory_space_constraint(operand, pltpu.HBM)
            for operand in (
                queries, keys, values, cotangent,
                query_gain.reshape(HEADS, HD), key_gain.reshape(HEADS, HD),
            )
        )
    )
    attended, query_grad, key_grad, value_grad, query_total, key_total = pl.pallas_call(
        settle,
        out_shape=(big, big, big, big, small, small),
        in_specs=[hbm] * 6,
        out_specs=(hbm,) * 6,
        scratch_shapes=[dma((6,))],
        compiler_params=pltpu.CompilerParams(vmem_limit_bytes=2**20),
        name="settle",
    )(*(pltpu.with_memory_space_constraint(result, pltpu.VMEM) for result in results))
    return (
        attended, query_grad, key_grad, value_grad,
        query_total.reshape(-1), key_total.reshape(-1),
    )


def solution(mesh):
    return jax.shard_map(
        body,
        mesh=mesh,
        in_specs=(
            P("col", "row", None),
            P("col", "row", None),
            P("col", "row", None),
            P(),
            P(),
            P("col", "row", None),
        ),
        out_specs=(
            P("col", "row", None),
            P("col", "row", None),
            P("col", "row", None),
            P("col", "row", None),
            P(),
            P(),
        ),
        check_vma=False,
    )
```

```python
import functools

import jax
import jax.numpy as jnp
from jax import lax
from jax.experimental import pallas as pl
from jax.experimental.pallas import tpu as pltpu
from jax.sharding import PartitionSpec as P

HEADS = 48
HD = 128
ROWS = 8
MINE = HEADS // ROWS
TOK = 128
LENGTH = ROWS * TOK
WIDE = MINE * HD
BLK = 256
NEAR = 8
FAR = 4
ORDER = (4, 3, 5, 2, 6, 1, 7)
EARLY = 2
FACTOR = HD**-0.5
LOG2E = 1.4426950408889634
MESH = pl.DeviceIdType.MESH


def nn(left, right):
    return lax.dot_general(left, right, (((1,), (0,)), ((), ())), preferred_element_type=jnp.float32)


def nt(left, right):
    return lax.dot_general(left, right, (((1,), (1,)), ((), ())), preferred_element_type=jnp.float32)


def normalise(entries):
    centred = entries - jnp.mean(entries, axis=-1, keepdims=True)
    inverse = lax.rsqrt(jnp.mean(centred * centred, axis=-1, keepdims=True) + 1e-06)
    return centred * inverse, inverse


def norm_back(side, hat, inverse, gain):
    upstream = side.astype(jnp.float32)
    scaled = upstream * gain
    result = inverse * (
        scaled
        - jnp.mean(scaled, axis=-1, keepdims=True)
        - hat * jnp.mean(scaled * hat, axis=-1, keepdims=True)
    )
    return result.astype(jnp.bfloat16), jnp.sum(upstream * hat, axis=0, keepdims=True)


def drain(ref, sem):
    pltpu.make_async_copy(ref, ref, sem).wait()


def kernel(
    q_ref, k_ref, v_ref, g_ref, qgain_hbm, kgain_hbm,
    att_ref, dq_ref, dk_ref, dv_ref, gq_ref, gk_ref,
    land, res, qhat, khat, qinv, kinv, qn, kn, knt, vt, dk_acc, dv_acc,
    part, land1, sum1, land2, sum2, land3, land4, total_q, total_k, qgain_ref, kgain_ref,
    f_send, f_recv, own_in, r_send, r_recv, own_out, g_send, g_recv, g_out, g_in, rings_here, from_left, from_right,
):
    me = lax.axis_index("row")
    col = lax.axis_index("col")
    near = lax.rem(col, NEAR)
    far = lax.div(col, NEAR)
    sources = (q_ref, k_ref, v_ref, g_ref)
    targets = (att_ref, dq_ref, dk_ref, dv_ref)

    def row_peer(d):
        return lax.rem(me + d, ROWS)

    def near_peer(d):
        return far * NEAR + lax.rem(near + d, NEAR)

    def far_peer(d):
        return lax.rem(far + d, FAR) * NEAR + near

    left, right = (row_peer(ROWS - 1), col), (row_peer(1), col)
    plane_peers = [(me, near_peer(d)) for d in range(1, NEAR)]
    plane_peers += [(me, far_peer(d)) for d in range(1, FAR)]

    barrier = pltpu.get_barrier_semaphore()
    for device in (left, right):
        pl.semaphore_signal(barrier, inc=1, device_id=device, device_id_type=MESH)

    @pl.when(me == 0)
    def _():
        for device in plane_peers:
            pl.semaphore_signal(barrier, inc=1, device_id=device, device_id_type=MESH)
        pl.semaphore_wait(barrier, 2 + len(plane_peers))

    @pl.when(me != 0)
    def _():
        pl.semaphore_wait(barrier, 2)

    def columns(owner, h):
        return pl.ds(pl.multiple_of(owner * WIDE + h * HD, HD), HD)

    def rows(owner):
        return pl.ds(pl.multiple_of(owner * TOK, TOK), TOK)

    def send_to(h, d):
        peer = row_peer(d)
        for t in range(4):
            pltpu.make_async_remote_copy(
                src_ref=sources[t].at[0, :, columns(peer, h)],
                dst_ref=land.at[h, t, rows(me), :],
                send_sem=f_send,
                recv_sem=f_recv.at[h],
                device_id=(peer, col),
                device_id_type=MESH,
            ).start()

    for step in range(1, ROWS // 2):
        pl.semaphore_signal(from_left.at[step - 1], inc=1, device_id=right, device_id_type=MESH)
        if step < ROWS // 2 - 1:
            pl.semaphore_signal(from_right.at[step - 1], inc=1, device_id=left, device_id_type=MESH)
        send_to(0, step)
        send_to(0, ROWS - step)
        pl.semaphore_wait(from_left.at[step - 1], 1)
        if step < ROWS // 2 - 1:
            pl.semaphore_wait(from_right.at[step - 1], 1)
    send_to(0, ROWS // 2)

    def send_forward(h, carry):
        for d in ORDER:
            send_to(h, d)
        return carry

    lax.fori_loop(1, MINE, send_forward, 0)

    def fetch_own(h, carry):
        for t in range(4):
            pltpu.make_async_copy(
                sources[t].at[0, :, columns(me, h)], land.at[h, t, rows(me), :], own_in.at[h]
            ).start()
        return carry

    lax.fori_loop(0, MINE, fetch_own, 0)

    @pl.when(me == 0)
    def _():
        for device in plane_peers:
            pl.semaphore_signal(rings_here, inc=1, device_id=device, device_id_type=MESH)

    def send_back(h):
        for d in ORDER:
            peer = row_peer(d)
            for t in range(4):
                pltpu.make_async_remote_copy(
                    src_ref=res.at[h, t, rows(peer), :],
                    dst_ref=targets[t].at[0, :, columns(me, h)],
                    send_sem=r_send,
                    recv_sem=r_recv.at[t],
                    device_id=(peer, col),
                    device_id_type=MESH,
                ).start()
        for t in range(4):
            pltpu.make_async_copy(
                res.at[h, t, rows(me), :], targets[t].at[0, :, columns(me, h)], own_out
            ).start()

    pltpu.make_async_copy(qgain_hbm, qgain_ref, g_in.at[0]).start()
    pltpu.make_async_copy(kgain_hbm, kgain_ref, g_in.at[1]).start()
    part[...] = jnp.zeros_like(part)
    drain(qgain_ref, g_in.at[0])
    drain(kgain_ref, g_in.at[1])

    def one_head(h, carry):
        drain(land.at[h, :, pl.ds(0, LENGTH - TOK), :], f_recv.at[h])
        drain(land.at[h, :, pl.ds(0, TOK), :], own_in.at[h])
        gain_q = qgain_ref[pl.ds(me * MINE + h, 1), :]
        gain_k = kgain_ref[pl.ds(me * MINE + h, 1), :]
        hat, inverse = normalise(land[h, 0].astype(jnp.float32))
        qhat[...] = hat
        qinv[...] = inverse
        qn[...] = (hat * gain_q).astype(jnp.bfloat16)
        hat, inverse = normalise(land[h, 1].astype(jnp.float32))
        khat[...] = hat
        kinv[...] = inverse
        normed = hat * gain_k
        kn[...] = normed.astype(jnp.bfloat16)
        knt[...] = normed.T.astype(jnp.bfloat16)
        vt[...] = land[h, 2].astype(jnp.float32).T.astype(jnp.bfloat16)
        dk_acc[...] = jnp.zeros_like(dk_acc)
        dv_acc[...] = jnp.zeros_like(dv_acc)

        def block(b, total):
            mine = pl.ds(pl.multiple_of(b * BLK, BLK), BLK)
            q_blk = qn[mine, :]
            g_blk = land[h, 3, mine, :]
            raised = jnp.exp2(nt(kn[...], q_blk) * (FACTOR * LOG2E))
            weights = raised * (1.0 / jnp.sum(raised, axis=0, keepdims=True))
            low = weights.astype(jnp.bfloat16)
            res[h, 0, mine, :] = nn(vt[...], low).T.astype(jnp.bfloat16)
            dv_acc[...] += nn(low, g_blk)
            weights_grad = nt(land[h, 2], g_blk)
            inner = jnp.sum(weights * weights_grad, axis=0, keepdims=True)
            score_grad = (weights * (weights_grad - inner)).astype(jnp.bfloat16)
            dk_acc[...] += nn(score_grad, q_blk)
            side = (nn(knt[...], score_grad) * FACTOR).T.astype(jnp.bfloat16)
            grad, term = norm_back(side, qhat[mine, :], qinv[mine, :], gain_q)
            res[h, 1, mine, :] = grad
            return total + term

        sum_q = lax.fori_loop(0, LENGTH // BLK, block, jnp.zeros((1, HD), jnp.float32))
        res[h, 3] = dv_acc[...].astype(jnp.bfloat16)
        side = (dk_acc[...] * FACTOR).astype(jnp.bfloat16)
        grad, sum_k = norm_back(side, khat[...], kinv[...], gain_k)
        res[h, 2] = grad
        part[lax.div(h, 2), pl.ds(lax.rem(h, 2), 1), :] = sum_q
        part[MINE // 2 + lax.div(h, 2), pl.ds(lax.rem(h, 2), 1), :] = sum_k

        @pl.when(h < EARLY)
        def _():
            send_back(h)

        return carry

    lax.fori_loop(0, MINE, one_head, 0)

    @pl.when(me == 0)
    def _():
        pl.semaphore_wait(rings_here, len(plane_peers))
        for d in range(1, ROWS):
            pl.semaphore_signal(rings_here, inc=1, device_id=(row_peer(d), col), device_id_type=MESH)

    @pl.when(me != 0)
    def _():
        pl.semaphore_wait(rings_here, 1)

    def share(stage, source, slots, slot, device):
        pltpu.make_async_remote_copy(
            src_ref=source,
            dst_ref=slots.at[slot],
            send_sem=g_send.at[stage],
            recv_sem=g_recv.at[stage],
            device_id=device,
            device_id_type=MESH,
        ).start()

    def shared(stage, slots, count):
        drain(slots.at[pl.ds(0, count - 1)], g_recv.at[stage])

    for d in range(1, NEAR):
        share(0, part.at[lax.rem(near + d, NEAR)], land1, near, (me, near_peer(d)))
    land1[near] = part[near]
    send_back(2)
    shared(0, land1, NEAR)
    sum1[...] = jnp.sum(land1[...], axis=0)
    for d in range(1, FAR):
        share(1, sum1, land2, far, (me, far_peer(d)))
    land2[far] = sum1[...]
    send_back(3)
    shared(1, land2, FAR)
    sum2[...] = jnp.sum(land2[...], axis=0)
    for d in range(1, ROWS):
        share(2, sum2, land3, me, (row_peer(d), col))
    land3[me] = sum2[...]
    send_back(4)
    shared(2, land3, ROWS)
    for d in range(1, NEAR):
        share(3, land3, land4, near, (me, near_peer(d)))
    land4[near] = land3[...]
    send_back(5)
    shared(3, land4, NEAR)
    for r in range(ROWS):
        for h in range(0, MINE, 2):
            total_q[r * MINE + h : r * MINE + h + 2, :] = land4[h // 2, r]
            total_k[r * MINE + h : r * MINE + h + 2, :] = land4[(MINE + h) // 2, r]
    pltpu.make_async_copy(total_q, gq_ref, g_out.at[0]).start()
    pltpu.make_async_copy(total_k, gk_ref, g_out.at[1]).start()
    drain(total_q, g_out.at[0])
    drain(total_k, g_out.at[1])
    drain(land1.at[pl.ds(0, NEAR - 1)], g_send.at[0])
    drain(land2.at[pl.ds(0, FAR - 1)], g_send.at[1])
    drain(land3.at[pl.ds(0, ROWS - 1)], g_send.at[2])
    drain(land4.at[pl.ds(0, NEAR - 1)], g_send.at[3])
    drain(land.at[:, :, pl.ds(0, LENGTH - TOK), :], f_send)
    drain(res.at[:, :, pl.ds(0, LENGTH - TOK), :], r_send)
    drain(res.at[:, :, pl.ds(0, TOK), :], own_out)
    for t in range(4):
        drain(targets[t].at[0, :, pl.ds(0, HEADS * HD - WIDE)], r_recv.at[t])


def settle(*refs):
    sems = refs[-1]
    count = len(refs) // 2
    copies = [
        pltpu.make_async_copy(refs[i], refs[count + i], sems.at[i]) for i in range(count)
    ]
    for copy in copies:
        copy.start()
    for copy in copies:
        copy.wait()


def body(queries, keys, values, query_gain, key_gain, cotangent):
    big = jax.ShapeDtypeStruct(queries.shape, jnp.bfloat16)
    small = jax.ShapeDtypeStruct((HEADS, HD), jnp.float32)
    hbm = pl.BlockSpec(memory_space=pl.ANY)
    token_f32 = pltpu.VMEM((LENGTH, HD), jnp.float32)
    token_bf16 = pltpu.VMEM((LENGTH, HD), jnp.bfloat16)
    column = pltpu.VMEM((LENGTH, 1), jnp.float32)
    turned = pltpu.VMEM((HD, LENGTH), jnp.bfloat16)
    blocks = pltpu.VMEM((MINE, 4, LENGTH, HD), jnp.bfloat16)
    dma = pltpu.SemaphoreType.DMA
    held = pltpu.VMEM(queries.shape, jnp.bfloat16)
    held_small = pltpu.VMEM((HEADS, HD), jnp.float32)
    results = pl.pallas_call(
        kernel,
        out_shape=(held, held, held, held, held_small, held_small),
        in_specs=[hbm] * 6,
        out_specs=(hbm,) * 6,
        scratch_shapes=[
            blocks, blocks, token_f32, token_f32, column, column, token_bf16, token_bf16,
            turned, turned, token_f32, token_f32,
            pltpu.VMEM((NEAR, 2, HD), jnp.float32),
            pltpu.VMEM((NEAR, 2, HD), jnp.float32),
            pltpu.VMEM((2, HD), jnp.float32),
            pltpu.VMEM((FAR, 2, HD), jnp.float32),
            pltpu.VMEM((2, HD), jnp.float32),
            pltpu.VMEM((ROWS, 2, HD), jnp.float32),
            pltpu.VMEM((NEAR, ROWS, 2, HD), jnp.float32),
            pltpu.VMEM((HEADS, HD), jnp.float32),
            pltpu.VMEM((HEADS, HD), jnp.float32),
            pltpu.VMEM((HEADS, HD), jnp.float32),
            pltpu.VMEM((HEADS, HD), jnp.float32),
            dma, dma((MINE,)), dma((MINE,)), dma, dma((4,)), dma, dma((4,)), dma((4,)), dma((2,)), dma((2,)),
            pltpu.SemaphoreType.REGULAR,
            pltpu.SemaphoreType.REGULAR((ROWS // 2 - 1,)),
            pltpu.SemaphoreType.REGULAR((ROWS // 2 - 2,)),
        ],
        compiler_params=pltpu.CompilerParams(
            collective_id=0, has_side_effects=True, vmem_limit_bytes=40 * 2**20
        ),
        cost_estimate=pl.CostEstimate(
            flops=12 * MINE * LENGTH * LENGTH * HD,
            bytes_accessed=16 * TOK * HEADS * HD,
            transcendentals=MINE * LENGTH * LENGTH,
        ),
        name="attention_exchange",
    )(
        *(
            pltpu.with_memory_space_constraint(operand, pltpu.HBM)
            for operand in (
                queries, keys, values, cotangent,
                query_gain.reshape(HEADS, HD), key_gain.reshape(HEADS, HD),
            )
        )
    )
    attended, query_grad, key_grad, value_grad, query_total, key_total = pl.pallas_call(
        settle,
        out_shape=(big, big, big, big, small, small),
        in_specs=[hbm] * 6,
        out_specs=(hbm,) * 6,
        scratch_shapes=[dma((6,))],
        compiler_params=pltpu.CompilerParams(vmem_limit_bytes=2**20),
        name="settle",
    )(*(pltpu.with_memory_space_constraint(result, pltpu.VMEM) for result in results))
    return (
        attended, query_grad, key_grad, value_grad,
        query_total.reshape(-1), key_total.reshape(-1),
    )


def solution(mesh):
    return jax.shard_map(
        body,
        mesh=mesh,
        in_specs=(
            P("col", "row", None),
            P("col", "row", None),
            P("col", "row", None),
            P(),
            P(),
            P("col", "row", None),
        ),
        out_specs=(
            P("col", "row", None),
            P("col", "row", None),
            P("col", "row", None),
            P("col", "row", None),
            P(),
            P(),
        ),
        check_vma=False,
    )
```

```python
import functools

import jax
import jax.numpy as jnp
from jax import lax
from jax.experimental import pallas as pl
from jax.experimental.pallas import tpu as pltpu
from jax.sharding import PartitionSpec as P

HEADS = 48
HD = 128
ROWS = 8
MINE = HEADS // ROWS
TOK = 128
LENGTH = ROWS * TOK
WIDE = MINE * HD
BLK = 256
NEAR = 8
FAR = 4
ORDER = (4, 3, 5, 2, 6, 1, 7)
EARLY = 2
FACTOR = HD**-0.5
LOG2E = 1.4426950408889634
MESH = pl.DeviceIdType.MESH


def nn(left, right):
    return lax.dot_general(left, right, (((1,), (0,)), ((), ())), preferred_element_type=jnp.float32)


def nt(left, right):
    return lax.dot_general(left, right, (((1,), (1,)), ((), ())), preferred_element_type=jnp.float32)


def normalise(entries):
    centred = entries - jnp.mean(entries, axis=-1, keepdims=True)
    inverse = lax.rsqrt(jnp.mean(centred * centred, axis=-1, keepdims=True) + 1e-06)
    return centred * inverse, inverse


def norm_back(side, hat, inverse, gain):
    upstream = side.astype(jnp.float32)
    scaled = upstream * gain
    result = inverse * (
        scaled
        - jnp.mean(scaled, axis=-1, keepdims=True)
        - hat * jnp.mean(scaled * hat, axis=-1, keepdims=True)
    )
    return result.astype(jnp.bfloat16), jnp.sum(upstream * hat, axis=0, keepdims=True)


def drain(ref, sem):
    pltpu.make_async_copy(ref, ref, sem).wait()


def kernel(
    q_ref, k_ref, v_ref, g_ref, qgain_hbm, kgain_hbm,
    back_ref, gq_ref, gk_ref,
    land, res, qhat, khat, qinv, kinv, qn, kn, knt, vt, dk_acc, dv_acc,
    part, land1, sum1, land2, sum2, land3, land4, total_q, total_k, qgain_ref, kgain_ref,
    f_send, f_recv, own_in, r_send, r_recv, own_out, g_send, g_recv, g_out, g_in, rings_here, from_left, from_right,
):
    me = lax.axis_index("row")
    col = lax.axis_index("col")
    near = lax.rem(col, NEAR)
    far = lax.div(col, NEAR)
    sources = (q_ref, k_ref, v_ref, g_ref)

    def row_peer(d):
        return lax.rem(me + d, ROWS)

    def near_peer(d):
        return far * NEAR + lax.rem(near + d, NEAR)

    def far_peer(d):
        return lax.rem(far + d, FAR) * NEAR + near

    left, right = (row_peer(ROWS - 1), col), (row_peer(1), col)
    plane_peers = [(me, near_peer(d)) for d in range(1, NEAR)]
    plane_peers += [(me, far_peer(d)) for d in range(1, FAR)]

    barrier = pltpu.get_barrier_semaphore()
    for device in (left, right):
        pl.semaphore_signal(barrier, inc=1, device_id=device, device_id_type=MESH)

    @pl.when(me == 0)
    def _():
        for device in plane_peers:
            pl.semaphore_signal(barrier, inc=1, device_id=device, device_id_type=MESH)
        pl.semaphore_wait(barrier, 2 + len(plane_peers))

    @pl.when(me != 0)
    def _():
        pl.semaphore_wait(barrier, 2)

    def columns(owner, h):
        return pl.ds(pl.multiple_of(owner * WIDE + h * HD, HD), HD)

    def rows(owner):
        return pl.ds(pl.multiple_of(owner * TOK, TOK), TOK)

    def send_to(h, d):
        peer = row_peer(d)
        for t in range(4):
            pltpu.make_async_remote_copy(
                src_ref=sources[t].at[0, :, columns(peer, h)],
                dst_ref=land.at[h, t, rows(me), :],
                send_sem=f_send,
                recv_sem=f_recv.at[h],
                device_id=(peer, col),
                device_id_type=MESH,
            ).start()

    for step in range(1, ROWS // 2):
        pl.semaphore_signal(from_left.at[step - 1], inc=1, device_id=right, device_id_type=MESH)
        if step < ROWS // 2 - 1:
            pl.semaphore_signal(from_right.at[step - 1], inc=1, device_id=left, device_id_type=MESH)
        send_to(0, step)
        send_to(0, ROWS - step)
        pl.semaphore_wait(from_left.at[step - 1], 1)
        if step < ROWS // 2 - 1:
            pl.semaphore_wait(from_right.at[step - 1], 1)
    send_to(0, ROWS // 2)

    def send_forward(h, carry):
        for d in ORDER:
            send_to(h, d)
        return carry

    lax.fori_loop(1, MINE, send_forward, 0)

    def fetch_own(h, carry):
        for t in range(4):
            pltpu.make_async_copy(
                sources[t].at[0, :, columns(me, h)], land.at[h, t, rows(me), :], own_in.at[h]
            ).start()
        return carry

    lax.fori_loop(0, MINE, fetch_own, 0)

    @pl.when(me == 0)
    def _():
        for device in plane_peers:
            pl.semaphore_signal(rings_here, inc=1, device_id=device, device_id_type=MESH)

    def send_back(h):
        for d in ORDER:
            peer = row_peer(d)
            pltpu.make_async_remote_copy(
                src_ref=res.at[h, :, rows(peer), :],
                dst_ref=back_ref.at[:, :, columns(me, h)],
                send_sem=r_send,
                recv_sem=r_recv,
                device_id=(peer, col),
                device_id_type=MESH,
            ).start()
        pltpu.make_async_copy(
            res.at[h, :, rows(me), :], back_ref.at[:, :, columns(me, h)], own_out
        ).start()

    pltpu.make_async_copy(qgain_hbm, qgain_ref, g_in.at[0]).start()
    pltpu.make_async_copy(kgain_hbm, kgain_ref, g_in.at[1]).start()
    part[...] = jnp.zeros_like(part)
    drain(qgain_ref, g_in.at[0])
    drain(kgain_ref, g_in.at[1])

    def one_head(h, carry):
        drain(land.at[h, :, pl.ds(0, LENGTH - TOK), :], f_recv.at[h])
        drain(land.at[h, :, pl.ds(0, TOK), :], own_in.at[h])
        gain_q = qgain_ref[pl.ds(me * MINE + h, 1), :]
        gain_k = kgain_ref[pl.ds(me * MINE + h, 1), :]
        hat, inverse = normalise(land[h, 0].astype(jnp.float32))
        qhat[...] = hat
        qinv[...] = inverse
        qn[...] = (hat * gain_q).astype(jnp.bfloat16)
        hat, inverse = normalise(land[h, 1].astype(jnp.float32))
        khat[...] = hat
        kinv[...] = inverse
        normed = hat * gain_k
        kn[...] = normed.astype(jnp.bfloat16)
        knt[...] = normed.T.astype(jnp.bfloat16)
        vt[...] = land[h, 2].astype(jnp.float32).T.astype(jnp.bfloat16)
        dk_acc[...] = jnp.zeros_like(dk_acc)
        dv_acc[...] = jnp.zeros_like(dv_acc)

        def block(b, total):
            mine = pl.ds(pl.multiple_of(b * BLK, BLK), BLK)
            q_blk = qn[mine, :]
            g_blk = land[h, 3, mine, :]
            raised = jnp.exp2(nt(kn[...], q_blk) * (FACTOR * LOG2E))
            weights = raised * (1.0 / jnp.sum(raised, axis=0, keepdims=True))
            low = weights.astype(jnp.bfloat16)
            res[h, 0, mine, :] = nn(vt[...], low).T.astype(jnp.bfloat16)
            dv_acc[...] += nn(low, g_blk)
            weights_grad = nt(land[h, 2], g_blk)
            inner = jnp.sum(weights * weights_grad, axis=0, keepdims=True)
            score_grad = (weights * (weights_grad - inner)).astype(jnp.bfloat16)
            dk_acc[...] += nn(score_grad, q_blk)
            side = (nn(knt[...], score_grad) * FACTOR).T.astype(jnp.bfloat16)
            grad, term = norm_back(side, qhat[mine, :], qinv[mine, :], gain_q)
            res[h, 1, mine, :] = grad
            return total + term

        sum_q = lax.fori_loop(0, LENGTH // BLK, block, jnp.zeros((1, HD), jnp.float32))
        res[h, 3] = dv_acc[...].astype(jnp.bfloat16)
        side = (dk_acc[...] * FACTOR).astype(jnp.bfloat16)
        grad, sum_k = norm_back(side, khat[...], kinv[...], gain_k)
        res[h, 2] = grad
        part[lax.div(h, 2), pl.ds(lax.rem(h, 2), 1), :] = sum_q
        part[MINE // 2 + lax.div(h, 2), pl.ds(lax.rem(h, 2), 1), :] = sum_k

        @pl.when(h < EARLY)
        def _():
            send_back(h)

        return carry

    lax.fori_loop(0, MINE, one_head, 0)

    @pl.when(me == 0)
    def _():
        pl.semaphore_wait(rings_here, len(plane_peers))
        for d in range(1, ROWS):
            pl.semaphore_signal(rings_here, inc=1, device_id=(row_peer(d), col), device_id_type=MESH)

    @pl.when(me != 0)
    def _():
        pl.semaphore_wait(rings_here, 1)

    def share(stage, source, slots, slot, device):
        pltpu.make_async_remote_copy(
            src_ref=source,
            dst_ref=slots.at[slot],
            send_sem=g_send.at[stage],
            recv_sem=g_recv.at[stage],
            device_id=device,
            device_id_type=MESH,
        ).start()

    def shared(stage, slots, count):
        drain(slots.at[pl.ds(0, count - 1)], g_recv.at[stage])

    for d in range(1, NEAR):
        share(0, part.at[lax.rem(near + d, NEAR)], land1, near, (me, near_peer(d)))
    land1[near] = part[near]
    send_back(2)
    shared(0, land1, NEAR)
    sum1[...] = jnp.sum(land1[...], axis=0)
    for d in range(1, FAR):
        share(1, sum1, land2, far, (me, far_peer(d)))
    land2[far] = sum1[...]
    send_back(3)
    shared(1, land2, FAR)
    sum2[...] = jnp.sum(land2[...], axis=0)
    for d in range(1, ROWS):
        share(2, sum2, land3, me, (row_peer(d), col))
    land3[me] = sum2[...]
    send_back(4)
    shared(2, land3, ROWS)
    for d in range(1, NEAR):
        share(3, land3, land4, near, (me, near_peer(d)))
    land4[near] = land3[...]
    send_back(5)
    shared(3, land4, NEAR)
    for r in range(ROWS):
        for h in range(0, MINE, 2):
            total_q[r * MINE + h : r * MINE + h + 2, :] = land4[h // 2, r]
            total_k[r * MINE + h : r * MINE + h + 2, :] = land4[(MINE + h) // 2, r]
    pltpu.make_async_copy(total_q, gq_ref, g_out.at[0]).start()
    pltpu.make_async_copy(total_k, gk_ref, g_out.at[1]).start()
    drain(total_q, g_out.at[0])
    drain(total_k, g_out.at[1])
    drain(land1.at[pl.ds(0, NEAR - 1)], g_send.at[0])
    drain(land2.at[pl.ds(0, FAR - 1)], g_send.at[1])
    drain(land3.at[pl.ds(0, ROWS - 1)], g_send.at[2])
    drain(land4.at[pl.ds(0, NEAR - 1)], g_send.at[3])
    drain(land.at[:, :, pl.ds(0, LENGTH - TOK), :], f_send)
    drain(res.at[:, :, pl.ds(0, LENGTH - TOK), :], r_send)
    drain(res.at[:, :, pl.ds(0, TOK), :], own_out)
    drain(back_ref.at[:, :, pl.ds(0, HEADS * HD - WIDE)], r_recv)


def settle(back_ref, gq_ref, gk_ref, *rest):
    outs, sems = rest[:-1], rest[-1]
    held = [back_ref.at[pl.ds(t, 1)] for t in range(4)] + [gq_ref, gk_ref]
    copies = [pltpu.make_async_copy(held[i], outs[i], sems.at[i]) for i in range(6)]
    for copy in copies:
        copy.start()
    for copy in copies:
        copy.wait()


def body(queries, keys, values, query_gain, key_gain, cotangent):
    big = jax.ShapeDtypeStruct(queries.shape, jnp.bfloat16)
    small = jax.ShapeDtypeStruct((HEADS, HD), jnp.float32)
    hbm = pl.BlockSpec(memory_space=pl.ANY)
    token_f32 = pltpu.VMEM((LENGTH, HD), jnp.float32)
    token_bf16 = pltpu.VMEM((LENGTH, HD), jnp.bfloat16)
    column = pltpu.VMEM((LENGTH, 1), jnp.float32)
    turned = pltpu.VMEM((HD, LENGTH), jnp.bfloat16)
    blocks = pltpu.VMEM((MINE, 4, LENGTH, HD), jnp.bfloat16)
    dma = pltpu.SemaphoreType.DMA
    held = pltpu.VMEM((4, TOK, HEADS * HD), jnp.bfloat16)
    held_small = pltpu.VMEM((HEADS, HD), jnp.float32)
    results = pl.pallas_call(
        kernel,
        out_shape=(held, held_small, held_small),
        in_specs=[hbm] * 6,
        out_specs=(hbm,) * 3,
        scratch_shapes=[
            blocks, blocks, token_f32, token_f32, column, column, token_bf16, token_bf16,
            turned, turned, token_f32, token_f32,
            pltpu.VMEM((NEAR, 2, HD), jnp.float32),
            pltpu.VMEM((NEAR, 2, HD), jnp.float32),
            pltpu.VMEM((2, HD), jnp.float32),
            pltpu.VMEM((FAR, 2, HD), jnp.float32),
            pltpu.VMEM((2, HD), jnp.float32),
            pltpu.VMEM((ROWS, 2, HD), jnp.float32),
            pltpu.VMEM((NEAR, ROWS, 2, HD), jnp.float32),
            pltpu.VMEM((HEADS, HD), jnp.float32),
            pltpu.VMEM((HEADS, HD), jnp.float32),
            pltpu.VMEM((HEADS, HD), jnp.float32),
            pltpu.VMEM((HEADS, HD), jnp.float32),
            dma, dma((MINE,)), dma((MINE,)), dma, dma, dma, dma((4,)), dma((4,)), dma((2,)), dma((2,)),
            pltpu.SemaphoreType.REGULAR,
            pltpu.SemaphoreType.REGULAR((ROWS // 2 - 1,)),
            pltpu.SemaphoreType.REGULAR((ROWS // 2 - 2,)),
        ],
        compiler_params=pltpu.CompilerParams(
            collective_id=0, has_side_effects=True, vmem_limit_bytes=40 * 2**20
        ),
        cost_estimate=pl.CostEstimate(
            flops=12 * MINE * LENGTH * LENGTH * HD,
            bytes_accessed=16 * TOK * HEADS * HD,
            transcendentals=MINE * LENGTH * LENGTH,
        ),
        name="attention_exchange",
    )(
        *(
            pltpu.with_memory_space_constraint(operand, pltpu.HBM)
            for operand in (
                queries, keys, values, cotangent,
                query_gain.reshape(HEADS, HD), key_gain.reshape(HEADS, HD),
            )
        )
    )
    attended, query_grad, key_grad, value_grad, query_total, key_total = pl.pallas_call(
        settle,
        out_shape=(big, big, big, big, small, small),
        in_specs=[hbm] * 3,
        out_specs=(hbm,) * 6,
        scratch_shapes=[dma((6,))],
        compiler_params=pltpu.CompilerParams(vmem_limit_bytes=2**20),
        name="settle",
    )(*(pltpu.with_memory_space_constraint(result, pltpu.VMEM) for result in results))
    return (
        attended, query_grad, key_grad, value_grad,
        query_total.reshape(-1), key_total.reshape(-1),
    )


def solution(mesh):
    return jax.shard_map(
        body,
        mesh=mesh,
        in_specs=(
            P("col", "row", None),
            P("col", "row", None),
            P("col", "row", None),
            P(),
            P(),
            P("col", "row", None),
        ),
        out_specs=(
            P("col", "row", None),
            P("col", "row", None),
            P("col", "row", None),
            P("col", "row", None),
            P(),
            P(),
        ),
        check_vma=False,
    )
```
